32 devices in a mesh: seq: 4 (over z), files: 8 (over y, x, core).
Axes of the slice: x: 2, y: 2, z: 4, core: 2. Of those that a mesh axis runs over, the one named last changes fastest.
Arguments:
- q_lin: bfloat16 [8, 1024, 320], P('files', 'seq'), may hold values from -6 to 6
- k_lin: bfloat16 [8, 1024, 320], P('files', 'seq'), may hold values from -6 to 6
- v_lin: bfloat16 [8, 1024, 2560], P('files', 'seq'), may hold values from -6 to 6
- q_soft: bfloat16 [8, 1024, 1280], P('files', 'seq'), may hold values from -48 to 48
- k_soft: bfloat16 [8, 1024, 1280], P('files', 'seq'), may hold values from -6 to 6
- v_soft: bfloat16 [8, 1024, 1280], P('files', 'seq'), may hold values from -6 to 6
- import_ids: int32 [8, 4, 2], P('files', 'seq'), may hold values from -1 to 15, as said below
- import_counts: int32 [8, 4], P('files', 'seq'), may hold values from 1 to 2, as said below
Outputs:
- lin_out: bfloat16 [8, 1024, 2560], P('files', 'seq')
- soft_out: bfloat16 [8, 1024, 1280], P('files', 'seq')
The draws below stay inside these ranges and needn't reach their ends.
Inputs may be any that keep to these rules, and one draw needn't show every extreme that they name: `import_ids`: entries before the count name distinct file groups other than the reader's own, entry = group * 2 + block; entries from the count on are -1. For each sequence shard index, some file group is listed before the count by every other file group's list of that index. `import_counts`: some sequence shard lists 2 blocks.
All inputs are finite; a program needn't handle non-finite values.
Results may differ from the reference program's by a relative error of at most 0.005.
Values may be sent and summed in bfloat16 or wider, within the bound.
A program may use at most 192 MiB of HBM per device.

```python
import math
import jax
import jax.numpy as jnp
import numpy as np
from jax import lax

D = 2560
HEADS = 20
FEAT = 16
FEATS = 153
SM_HEADS = 10
SM_HD = 128
SM_W = 1280
BLK = 128
TOK_DEV = 256
MAXB = 2
BLOCKS_DEV = 2
GROUPS = 8
SHARDS = 4
SEQ_LEN = 1024


def score_pair(key):
    key_keys = jax.random.fold_in(key, 101)
    key_query = jax.random.fold_in(key, 102)
    shape = (GROUPS, SEQ_LEN, SM_W)
    keys = jnp.clip(jax.random.normal(key_keys, shape, jnp.float32), -6.0, 6.0)
    query = jnp.clip(jax.random.normal(key_query, shape, jnp.float32), -6.0, 6.0)
    return (query, keys)


def draw_q_soft(key, part):
    return score_pair(key)[0].astype(jnp.bfloat16)


def draw_k_soft(key, part):
    return score_pair(key)[1].astype(jnp.bfloat16)


def import_lists(key):
    base = jax.random.fold_in(key, 7)
    key_order = jax.random.fold_in(base, 1)
    key_block = jax.random.fold_in(base, 2)
    key_light = jax.random.fold_in(base, 4)
    key_place = jax.random.fold_in(base, 5)
    key_hot = jax.random.fold_in(base, 6)
    key_slot = jax.random.fold_in(base, 8)
    others = GROUPS - 1
    scores = jax.random.randint(key_order, (GROUPS, SHARDS, others), 0, 1 << 20) * others + jnp.arange(others)
    hot_owner = jax.random.randint(key_hot, (SHARDS,), 0, GROUPS)
    target = (hot_owner[None, :] - jnp.arange(GROUPS)[:, None] - 1) % GROUPS
    scores = jnp.where(jnp.arange(others)[None, None, :] == target[..., None], -1, scores)
    order = jnp.argsort(scores, axis=-1, stable=True)[..., :MAXB]
    low = 3 * MAXB // 4
    counts = low + jax.random.randint(key_light, (GROUPS, SHARDS), 0, MAXB - low + 1)
    counts = counts.reshape(-1)
    place = jax.random.randint(key_place, (), 0, GROUPS * SHARDS)
    counts = counts.at[place].set(MAXB).reshape(GROUPS, SHARDS).astype(jnp.int32)
    slot = jax.random.randint(key_slot, (GROUPS, SHARDS), 0, 1 << 20) % counts
    position = jnp.arange(MAXB)[None, None, :]
    source = jnp.where(position == 0, slot[..., None], jnp.where(position == slot[..., None], 0, position))
    order = jnp.take_along_axis(order, source, axis=-1)
    owner = (jnp.arange(GROUPS)[:, None, None] + 1 + order) % GROUPS
    block = jax.random.randint(key_block, (GROUPS, SHARDS, MAXB), 0, BLOCKS_DEV)
    entries = owner * BLOCKS_DEV + block
    entries = jnp.where(jnp.arange(MAXB) < counts[..., None], entries, -1).astype(jnp.int32)
    return (entries, counts)


def draw_import_ids(key, part):
    return import_lists(key)[0]


def draw_import_counts(key, part):
    return import_lists(key)[1]


def shard_levels(stream_key, shape, shards, low, largest):
    def one(dim, parts):
        steps = jax.random.uniform(jax.random.fold_in(jax.random.fold_in(stream_key, 6), dim), (parts,), jnp.float32, low / len(shards), largest / len(shards))
        return jnp.repeat(jnp.exp(steps), shape[dim] // parts).reshape((-1,) + (1,) * (len(shape) - dim - 1))

    factor_of = one(*shards[0])
    for cut in shards[1:]:
        factor_of = factor_of * one(*cut)
    return factor_of


def noise(own_key, dims, deviation, limit, cuts=(), held_as=jnp.bfloat16):
    values = jax.random.normal(own_key, dims, jnp.float32) * deviation
    if len(cuts) > 0:
        values = shard_levels(own_key, dims, cuts, -0.22, 0.18) * values
    return jnp.clip(values, min=-limit, max=limit).astype(held_as)


def setup_inputs(seed: int = 0) -> dict:
    streams_of = jax.random.split(jax.random.key(seed), 9)
    q_lin = noise(streams_of[0], (GROUPS, SEQ_LEN, HEADS * FEAT), 1.0, 6.0, ((0, 8), (1, 4)))
    k_lin = noise(streams_of[1], (GROUPS, SEQ_LEN, HEADS * FEAT), 1.0, 6.0, ((0, 8), (1, 4)))
    v_lin = noise(streams_of[2], (GROUPS, SEQ_LEN, D), 1.0, 6.0, ((0, 8), (1, 4)))
    q_soft = draw_q_soft(jax.random.fold_in(streams_of[8], 71), 0)
    k_soft = draw_k_soft(jax.random.fold_in(streams_of[8], 71), 0)
    v_soft = noise(streams_of[5], (GROUPS, SEQ_LEN, SM_W), 1.0, 6.0, ((0, 8), (1, 4)))
    import_ids = draw_import_ids(jax.random.fold_in(streams_of[8], 71), 0)
    import_counts = draw_import_counts(jax.random.fold_in(streams_of[8], 71), 0)
    return dict(q_lin=q_lin, k_lin=k_lin, v_lin=v_lin, q_soft=q_soft, k_soft=k_soft, v_soft=v_soft, import_ids=import_ids, import_counts=import_counts)


inv_root_two = 0.7071067811865476
highest_precision = lax.Precision.HIGHEST

def feature_map(inputs):
    count_in = inputs.shape[-1]
    rows, cols = np.triu_indices(count_in)
    factor = np.where(rows == cols, inv_root_two, 1.0).astype(np.float32)
    quadratic = inputs[..., rows] * inputs[..., cols] * factor
    ones = jnp.ones(inputs.shape[:-1] + (1,), inputs.dtype)
    return jnp.concatenate([ones, inputs, quadratic], axis=-1)

def rounded(values):
    return lax.optimization_barrier(values.astype(jnp.bfloat16)).astype(jnp.float32)

def linear_group(inputs):
    query_rows, key_rows, value_rows = inputs
    head_dim = D // HEADS
    nblocks = SEQ_LEN // BLK
    feat_q = feature_map(query_rows.astype(jnp.float32).reshape(SEQ_LEN, HEADS, FEAT) * 0.5).astype(jnp.bfloat16)
    feat_k = feature_map(key_rows.astype(jnp.float32).reshape(SEQ_LEN, HEADS, FEAT) * 0.5).astype(jnp.bfloat16)
    block_qs = feat_q.reshape(nblocks, BLK, HEADS, FEATS)
    block_ks = feat_k.reshape(nblocks, BLK, HEADS, FEATS)
    block_vs = value_rows.reshape(nblocks, BLK, HEADS, head_dim)
    causal_masking = jnp.tril(jnp.ones((BLK, BLK), jnp.float32))

    def advance(carry, block):
        running_state, norm_sum = carry
        query_tile_rows = block[0].astype(jnp.float32)
        key_tile_rows = block[1].astype(jnp.float32)
        value_tile_rows = block[2].astype(jnp.float32)
        weight_matrix = jnp.einsum('evy,ivy->vei', query_tile_rows, key_tile_rows, precision=highest_precision) * causal_masking
        numerator = jnp.einsum('hqk,khd->qhd', rounded(weight_matrix), value_tile_rows, precision=highest_precision)
        numerator = numerator + jnp.einsum('qhf,hfd->qhd', query_tile_rows, running_state, precision=highest_precision)
        denominator = lax.optimization_barrier(jnp.sum(weight_matrix, axis=-1)).T + jnp.einsum('qhf,hf->qh', query_tile_rows, norm_sum, precision=highest_precision)
        output = (numerator / denominator[..., None]).astype(jnp.bfloat16)
        running_state = running_state + jnp.einsum('sir,sig->irg', key_tile_rows, value_tile_rows, precision=highest_precision)
        norm_sum = norm_sum + lax.optimization_barrier(jnp.sum(key_tile_rows, axis=0))
        return ((running_state, norm_sum), output)
    start = (jnp.zeros((HEADS, FEATS, head_dim), jnp.float32), jnp.zeros((HEADS, FEATS), jnp.float32))
    final, outputs = lax.scan(advance, start, (block_qs, block_ks, block_vs))
    return outputs.reshape(SEQ_LEN, D)

def reference(q_lin, k_lin, v_lin, q_soft, k_soft, v_soft, import_ids, import_counts):
    lin_out = lax.map(linear_group, (q_lin, k_lin, v_lin))
    key_all = k_soft.reshape(GROUPS, SHARDS, BLOCKS_DEV, BLK, SM_W)
    value_all = v_soft.reshape(GROUPS, SHARDS, BLOCKS_DEV, BLK, SM_W)
    scale = 1.0 / math.sqrt(SM_HD)

    def soft_group(inputs):
        query_rows, key_rows, value_rows, id_rows, counts = inputs
        query5 = query_rows.astype(jnp.float32).reshape(SHARDS, BLOCKS_DEV, BLK, SM_HEADS, SM_HD)
        own_keys = key_rows.astype(jnp.float32).reshape(SHARDS, BLOCKS_DEV, BLK, SM_HEADS, SM_HD)
        own_vals = value_rows.astype(jnp.float32).reshape(SHARDS, BLOCKS_DEV, BLK, SM_HEADS, SM_HD)
        own_scores = jnp.einsum('sbqhd,sbkhd->shbqk', query5, own_keys, precision=highest_precision) * scale
        own_scores = own_scores.reshape(SHARDS, SM_HEADS, TOK_DEV, BLK)
        safe_ids = jnp.maximum(id_rows, 0)
        owner = safe_ids // BLOCKS_DEV
        within = safe_ids % BLOCKS_DEV
        shard_index = jnp.arange(SHARDS)[:, None]
        imp_keys = key_all[owner, shard_index, within].astype(jnp.float32).reshape(SHARDS, MAXB * BLK, SM_HEADS, SM_HD)
        imp_vals = value_all[owner, shard_index, within].astype(jnp.float32).reshape(SHARDS, MAXB * BLK, SM_HEADS, SM_HD)
        query4 = query5.reshape(SHARDS, TOK_DEV, SM_HEADS, SM_HD)
        imp_scores = jnp.einsum('sqhd,skhd->shqk', query4, imp_keys, precision=highest_precision) * scale
        listed = jnp.repeat(jnp.arange(MAXB)[None, :] < counts[:, None], BLK, axis=1)
        imp_scores = jnp.where(listed[:, None, None, :], imp_scores, -jnp.inf)
        top = jnp.maximum(lax.optimization_barrier(jnp.max(own_scores, axis=-1)), lax.optimization_barrier(jnp.max(imp_scores, axis=-1)))
        own_prob = jnp.exp(own_scores - top[..., None])
        imp_prob = jnp.exp(imp_scores - top[..., None])
        total = lax.optimization_barrier(jnp.sum(own_prob, axis=-1)) + lax.optimization_barrier(jnp.sum(imp_prob, axis=-1))
        own_prob5 = rounded(own_prob).reshape(SHARDS, SM_HEADS, BLOCKS_DEV, BLK, BLK)
        own_num = jnp.einsum('shbqk,sbkhd->sbqhd', own_prob5, own_vals, precision=highest_precision)
        own_num = own_num.reshape(SHARDS, TOK_DEV, SM_HEADS, SM_HD)
        imp_num = jnp.einsum('shqk,skhd->sqhd', rounded(imp_prob), imp_vals, precision=highest_precision)
        output = (own_num + imp_num) / jnp.transpose(total, (0, 2, 1))[..., None]
        return output.astype(jnp.bfloat16).reshape(SEQ_LEN, SM_W)
    soft_out = lax.map(soft_group, (q_soft, k_soft, v_soft, import_ids, import_counts))
    return (lin_out, soft_out)
```

```python
import functools
import math

import jax
import jax.numpy as jnp
import numpy as np
from jax import lax
from jax.experimental import pallas as pl
from jax.experimental.pallas import tpu as pltpu
from jax.sharding import PartitionSpec as P

FEAT = 16
FEATS = 153
FPAD = 160
HD = 128
SM_HD = 128
BLK = 128
ROWS = 16
GROUP = 4
MESH = pl.DeviceIdType.MESH
F32 = jnp.float32
BF16 = jnp.bfloat16


def selectors():
    rows, cols = np.triu_indices(FEAT)
    lanes = np.arange(128) % FEAT
    first = np.zeros((FPAD, 128), np.float32)
    second = np.zeros((FPAD, 128), np.float32)
    second_q = np.zeros((FPAD, 128), np.float32)
    for i in range(FEAT):
        first[1 + i] = 0.5 * (lanes == i)
    for f, (i, j) in enumerate(zip(rows, cols)):
        first[1 + FEAT + f] = 0.5 * (lanes == i)
        second[1 + FEAT + f] = 0.5 * (lanes == j)
        second_q[1 + FEAT + f] = (0.25 if i == j else 0.5) * (lanes == j)
    for_k = np.concatenate([first, second])
    gap = np.zeros((256 - FPAD, 128), np.float32)
    for_q = np.concatenate([first, gap, second_q, gap])
    return for_k, for_q


def nt(a, b):
    return lax.dot_general(a, b, (((1,), (1,)), ((), ())), preferred_element_type=F32)


def nn(a, b):
    return lax.dot_general(a, b, (((1,), (0,)), ((), ())), preferred_element_type=F32)


def kernel(
    dims,
    q_ref, k_ref, v_ref, qs_ref, ks_hbm, vs_hbm, ids_ref, bias_ref, ek_ref, eq_ref,
    lin_ref, soft_ref,
    kv, pieces, outgoing, imp, tbl, tbl_s, qp, kp,
    local, s_send, s_recv, n_local, n_send, n_recv, own_num, own_max, own_sum,
    load_sem, ids_send, ids_recv, p1_send, p1_recv, p2_send, p2_recv,
    st_send, st_recv, nm_send, nm_recv, tbl_sem,
):
    n, nz, heads, sm_heads, blocks, maxb, kvs, cols = dims
    tokens = blocks * BLK
    me = lax.axis_index("files")
    z = lax.axis_index("seq")
    has_prev = z > 0
    has_next = z < nz - 1

    def peer(off):
        return lax.rem(me + off, n)

    def piece(p):
        if kvs == 2:
            col = lax.rem(p, n * ROWS // BLK)
            row = p // (n * ROWS // BLK)
            at_kv = pl.ds(0, 2)
        else:
            halves = n * ROWS // BLK // 2
            col = lax.rem(p, halves)
            row = p // (2 * halves)
            at_kv = pl.ds(lax.rem(p // halves, 2), 1)
        return at_kv, pl.ds(pl.multiple_of(row * ROWS, ROWS), ROWS), pl.ds(
            pl.multiple_of(col * cols, 128), cols
        )

    load_k = pltpu.make_async_copy(ks_hbm, kv.at[:, 0], load_sem.at[0])
    load_v = pltpu.make_async_copy(vs_hbm, kv.at[:, 1], load_sem.at[1])
    load_k.start()
    load_v.start()

    barrier = pltpu.get_barrier_semaphore()
    for off in range(1, n):
        pl.semaphore_signal(barrier, inc=1, device_id={"files": peer(off)}, device_id_type=MESH)

    @pl.when(has_prev)
    def _():
        pl.semaphore_signal(barrier, inc=1, device_id={"seq": z - 1}, device_id_type=MESH)

    @pl.when(has_next)
    def _():
        pl.semaphore_signal(barrier, inc=1, device_id={"seq": z + 1}, device_id_type=MESH)

    neighbours = (z + nz - 1) // nz + (2 * nz - 2 - z) // nz
    pl.semaphore_wait(barrier, n - 1 + neighbours)

    id_copies = []
    for off in range(1, n):
        c = pltpu.make_async_remote_copy(
            src_ref=ids_ref, dst_ref=tbl.at[me], send_sem=ids_send.at[off], recv_sem=ids_recv.at[off],
            device_id={"files": peer(off)}, device_id_type=MESH)
        c.start()
        id_copies.append(c)
    tbl[me] = ids_ref[...]
    load_k.wait()
    load_v.wait()
    first = []
    for off in range(1, n):
        to = peer(off)
        at_kv, at_row, at_col = piece(to)
        c = pltpu.make_async_remote_copy(
            src_ref=kv.at[:, at_kv, at_row, at_col], dst_ref=pieces.at[pl.ds(me * blocks, blocks)],
            send_sem=p1_send.at[off], recv_sem=p1_recv.at[off],
            device_id={"files": to}, device_id_type=MESH)
        c.start()
        first.append(c)
    at_kv, at_row, at_col = piece(me)
    mine = pltpu.make_async_copy(
        kv.at[:, at_kv, at_row, at_col], pieces.at[pl.ds(me * blocks, blocks)], load_sem.at[2])
    mine.start()

    lanes_in = heads * FEAT
    qp[...] = jnp.zeros_like(qp)
    kp[...] = jnp.zeros_like(kp)
    qp[:, :lanes_in] = q_ref[...]
    kp[:, :lanes_in] = k_ref[...]

    def head_tile(ref, h):
        lane = lax.broadcasted_iota(jnp.int32, (tokens, 128), 1)
        start = pl.multiple_of((h // 8) * 128, 128)
        tile = ref[:, pl.ds(start, 128)]
        low = lax.rem(h, 8) * FEAT
        inside = (lane >= low) & (lane < low + FEAT)
        return tile, jnp.where(inside, tile, jnp.zeros_like(tile))

    def lane_is(h, rows):
        return lax.broadcasted_iota(jnp.int32, (rows, 128), 1) == h

    def columns(h):
        return pl.ds(pl.multiple_of(h * HD, HD), HD)

    n_local[...] = jnp.zeros_like(n_local)

    def state_of(h):
        _, km = head_tile(kp, h)
        both = nt(ek_ref[...], km)
        row = lax.broadcasted_iota(jnp.int32, (FPAD, tokens), 0)
        feat = jnp.where(row == 0, 1.0, both[:FPAD]) * jnp.where(row < 1 + FEAT, 1.0, both[FPAD:])
        ones = jnp.where(lane_is(h, tokens), 1.0, 0.0).astype(BF16)
        right = jnp.concatenate([v_ref[:, columns(h)], ones], axis=1)
        made = nn(feat.astype(BF16), right)
        local[h] = made[:, :HD]
        return made[:, HD:]

    def states(i, carry):
        n_local[...] += state_of(2 * i) + state_of(2 * i + 1)
        return carry

    lax.fori_loop(0, heads // 2, states, 0)

    groups = heads // GROUP

    def norm_copy():
        return pltpu.make_async_remote_copy(
            src_ref=n_send, dst_ref=n_recv, send_sem=nm_send, recv_sem=nm_recv,
            device_id={"seq": lax.rem(z + 1, nz)}, device_id_type=MESH)

    def state_copy(g):
        at = pl.ds(g * GROUP, GROUP)
        return pltpu.make_async_remote_copy(
            src_ref=s_send.at[at], dst_ref=s_recv.at[at], send_sem=st_send.at[g], recv_sem=st_recv.at[g],
            device_id={"seq": lax.rem(z + 1, nz)}, device_id_type=MESH)

    @pl.when(z == 0)
    def _():
        n_recv[...] = jnp.zeros_like(n_recv)
        s_recv[...] = jnp.zeros_like(s_recv)

    @pl.when(has_prev)
    def _():
        norm_copy().wait_recv()

    @pl.when(has_next)
    def _():
        n_send[...] = n_recv[...] + n_local[...]
        norm_copy().start()

    def pass_on(g):
        at = pl.ds(g * GROUP, GROUP)

        @pl.when(has_prev)
        def _():
            state_copy(g).wait_recv()

        @pl.when(has_next)
        def _():
            s_send[at] = (s_recv[at].astype(F32) + local[at]).astype(BF16)
            state_copy(g).start()

    def lin_head(h, norms):
        _, qm = head_tile(qp, h)
        k_tile, _ = head_tile(kp, h)
        s = nt(qm, k_tile) * 0.25
        t_at = lax.broadcasted_iota(jnp.int32, (tokens, tokens), 0)
        s_at = lax.broadcasted_iota(jnp.int32, (tokens, tokens), 1)
        w = jnp.where(s_at <= t_at, 1.0 + s * (1.0 + 0.5 * s), 0.0)
        num = nn(w.astype(BF16), v_ref[:, columns(h)])
        both = nt(qm, eq_ref[...])
        lane = lax.broadcasted_iota(jnp.int32, (tokens, 256), 1)
        feat = jnp.where(lane == 0, 1.0, both[:, :256]) * jnp.where(lane < 1 + FEAT, 1.0, both[:, 256:])
        which = lane_is(h, FPAD) | lane_is(h + 64, FPAD)
        right = jnp.concatenate([s_recv[h], jnp.where(which, norms, jnp.zeros_like(norms))], axis=1)
        far = nn(feat[:, :FPAD].astype(BF16), right)
        den = jnp.sum(w, axis=1, keepdims=True) + jnp.sum(far[:, HD:], axis=1, keepdims=True)
        lin_ref[:, columns(h)] = ((num + far[:, :HD]) / den).astype(BF16)

    def lin_group(g):
        total = n_recv[...]
        high = total.astype(BF16)
        low = (total - high.astype(F32)).astype(BF16)
        norms = jnp.where(
            lax.broadcasted_iota(jnp.int32, (FPAD, 128), 1) < 64,
            high.astype(F32), pltpu.roll(low.astype(F32), 64, 1)).astype(BF16)

        def two(i, carry):
            lin_head(g * GROUP + 2 * i, norms)
            lin_head(g * GROUP + 2 * i + 1, norms)
            return carry

        lax.fori_loop(0, GROUP // 2, two, 0)

    scale = 1.0 / math.sqrt(SM_HD)

    def own_part(h, carry):
        at = columns(h)
        for b in range(blocks):
            rows = pl.ds(b * BLK, BLK)
            s = nt(qs_ref[rows, at], kv[b, 0, :, at]) * scale
            top = jnp.max(s, axis=1, keepdims=True)
            p = jnp.exp(s - top)
            own_max[h, rows] = top
            own_sum[h, rows] = jnp.sum(p, axis=1, keepdims=True)
            own_num[rows, at] = nn(p.astype(BF16), kv[b, 1, :, at])
        return carry

    def imported_part(h, carry):
        at = columns(h)
        keys = imp[:, 0, :, at].reshape(maxb * BLK, SM_HD)
        s = nt(qs_ref[:, at], keys) * scale + bias_ref[0:1, :]
        top = jnp.maximum(own_max[h], jnp.max(s, axis=1, keepdims=True))
        p = jnp.exp(s - top)
        before = jnp.exp(own_max[h] - top)
        total = own_sum[h] * before + jnp.sum(p, axis=1, keepdims=True)
        values = imp[:, 1, :, at].reshape(maxb * BLK, SM_HD)
        num = own_num[:, at] * before + nn(p.astype(BF16), values)
        soft_ref[:, at] = (num / total).astype(BF16)
        return carry

    second = []

    def exchange():
        for c in id_copies:
            c.wait_recv()
        to_smem = pltpu.make_async_copy(tbl, tbl_s, tbl_sem)
        to_smem.start()
        to_smem.wait()
        for c in first:
            c.wait_recv()
        mine.wait()
        at_kv, at_row, at_col = piece(me)
        for off in range(n):
            to = peer(off)
            for i in range(maxb):
                outgoing[off, i] = pieces[jnp.maximum(tbl_s[to, 0, i], 0)]
            there = imp.at[:, at_kv, at_row, at_col]
            if off == 0:
                c = pltpu.make_async_copy(outgoing.at[0], there, load_sem.at[3])
            else:
                c = pltpu.make_async_remote_copy(
                    src_ref=outgoing.at[off], dst_ref=there,
                    send_sem=p2_send.at[off], recv_sem=p2_recv.at[off],
                    device_id={"files": to}, device_id_type=MESH)
            c.start()
            second.append(c)

    pass_on(0)
    lax.fori_loop(0, sm_heads, own_part, 0)
    pass_on(1)
    exchange()
    for g in range(groups):
        if g >= 2:
            pass_on(g)
        lin_group(g)

    for c in second:
        if c is second[0]:
            c.wait()
        else:
            c.wait_recv()
    lax.fori_loop(0, sm_heads, imported_part, 0)

    for c in id_copies + first + second[1:]:
        c.wait_send()

    @pl.when(has_next)
    def _():
        norm_copy().wait_send()
        for g in range(groups):
            state_copy(g).wait_send()


def body(q_lin, k_lin, v_lin, q_soft, k_soft, v_soft, import_ids, import_counts):
    n, nz = lax.axis_size("files"), lax.axis_size("seq")
    tokens = q_lin.shape[1]
    blocks = tokens // BLK
    heads = q_lin.shape[2] // FEAT
    width, sm_w = v_lin.shape[2], q_soft.shape[2]
    sm_heads = sm_w // SM_HD
    maxb = import_ids.shape[2]
    col_parts = n * ROWS // BLK
    kvs = 2 if sm_w % (128 * col_parts) == 0 else 1
    cols = sm_w // col_parts if kvs == 2 else sm_w * 2 // col_parts
    lanes_in = -(-heads * FEAT // 128) * 128
    listed = jnp.arange(maxb) < import_counts[0, 0]
    ids = jnp.pad(jnp.where(listed, import_ids[0, 0], -1)[None], ((0, 7), (0, 128 - maxb)), constant_values=-1)
    bias = jnp.broadcast_to(
        jnp.repeat(jnp.where(listed, 0.0, -jnp.inf).astype(F32), BLK)[None], (8, maxb * BLK))
    for_k, for_q = selectors()
    dims = (n, nz, heads, sm_heads, blocks, maxb, kvs, cols)
    vmem = pl.BlockSpec(memory_space=pltpu.VMEM)
    hbm = pl.BlockSpec(memory_space=pl.ANY)
    dma = pltpu.SemaphoreType.DMA
    lin, soft = pl.pallas_call(
        functools.partial(kernel, dims),
        out_shape=(
            jax.ShapeDtypeStruct((tokens, width), BF16),
            jax.ShapeDtypeStruct((tokens, sm_w), BF16),
        ),
        in_specs=[vmem, vmem, vmem, vmem, hbm, hbm, vmem, vmem, vmem, vmem],
        out_specs=(vmem, vmem),
        scratch_shapes=[
            pltpu.VMEM((blocks, 2, BLK, sm_w), BF16),
            pltpu.VMEM((n * blocks, kvs, ROWS, cols), BF16),
            pltpu.VMEM((n, maxb, kvs, ROWS, cols), BF16),
            pltpu.VMEM((maxb, 2, BLK, sm_w), BF16),
            pltpu.VMEM((n, 8, 128), jnp.int32),
            pltpu.SMEM((n, 8, 128), jnp.int32),
            pltpu.VMEM((tokens, lanes_in), BF16),
            pltpu.VMEM((tokens, lanes_in), BF16),
            pltpu.VMEM((heads, FPAD, HD), F32),
            pltpu.VMEM((heads, FPAD, HD), BF16),
            pltpu.VMEM((heads, FPAD, HD), BF16),
            pltpu.VMEM((FPAD, HD), F32),
            pltpu.VMEM((FPAD, HD), F32),
            pltpu.VMEM((FPAD, HD), F32),
            pltpu.VMEM((tokens, sm_w), F32),
            pltpu.VMEM((sm_heads, tokens, 1), F32),
            pltpu.VMEM((sm_heads, tokens, 1), F32),
            dma((4,)), dma((n,)), dma((n,)), dma((n,)), dma((n,)), dma((n,)), dma((n,)),
            dma((heads // GROUP,)), dma((heads // GROUP,)), dma, dma, dma,
        ],
        compiler_params=pltpu.CompilerParams(
            collective_id=0, has_side_effects=True, vmem_limit_bytes=48 * 2**20),
    )(
        q_lin[0], k_lin[0], v_lin[0], q_soft[0],
        k_soft.reshape(blocks, BLK, sm_w), v_soft.reshape(blocks, BLK, sm_w),
        ids, bias, jnp.asarray(for_k, BF16), jnp.asarray(for_q, BF16),
    )
    return lin[None], soft[None]


def solution(mesh):
    row = P("files", "seq", None)
    return jax.shard_map(
        body,
        mesh=mesh,
        in_specs=(row,) * 7 + (P("files", "seq"),),
        out_specs=(row, row),
        check_vma=False,
    )
```

```python
import functools
import math

import jax
import jax.numpy as jnp
import numpy as np
from jax import lax
from jax.experimental import pallas as pl
from jax.experimental.pallas import tpu as pltpu
from jax.sharding import PartitionSpec as P

FEAT = 16
FEATS = 153
FPAD = 160
HD = 128
SM_HD = 128
BLK = 128
ROWS = 16
GROUP = 4
MESH = pl.DeviceIdType.MESH
F32 = jnp.float32
BF16 = jnp.bfloat16


def selectors():
    rows, cols = np.triu_indices(FEAT)
    lanes = np.arange(128) % FEAT
    first = np.zeros((FPAD, 128), np.float32)
    second = np.zeros((FPAD, 128), np.float32)
    second_q = np.zeros((FPAD, 128), np.float32)
    for i in range(FEAT):
        first[1 + i] = 0.5 * (lanes == i)
    for f, (i, j) in enumerate(zip(rows, cols)):
        first[1 + FEAT + f] = 0.5 * (lanes == i)
        second[1 + FEAT + f] = 0.5 * (lanes == j)
        second_q[1 + FEAT + f] = (0.25 if i == j else 0.5) * (lanes == j)
    for_k = np.concatenate([first, second])
    gap = np.zeros((256 - FPAD, 128), np.float32)
    for_q = np.concatenate([first, gap, second_q, gap])
    return for_k, for_q


def nt(a, b):
    return lax.dot_general(a, b, (((1,), (1,)), ((), ())), preferred_element_type=F32)


def nn(a, b):
    return lax.dot_general(a, b, (((1,), (0,)), ((), ())), preferred_element_type=F32)


def kernel(
    dims,
    q_hbm, k_hbm, v_hbm, qs_hbm, ks_hbm, vs_hbm, sel_hbm, ids_in, count_in,
    lin_ref, soft_ref,
    q_ref, k_ref, v_ref, qs_ref, sel_ref, ids_ref,
    kv, pieces, outgoing, imp, tbl, tbl_s, qp, kp,
    local, s_send, s_recv, n_local, n_send, n_recv, own_num, own_max, own_sum,
    load_sem, ids_send, ids_recv, p1_send, p1_recv, p2_send, p2_recv,
    st_send, st_recv, nm_send, nm_recv, tbl_sem,
):
    n, nz, heads, sm_heads, blocks, maxb, kvs, cols = dims
    tokens = blocks * BLK
    me = lax.axis_index("files")
    z = lax.axis_index("seq")
    has_prev = z > 0
    has_next = z < nz - 1

    def peer(off):
        return lax.rem(me + off, n)

    def piece(p):
        if kvs == 2:
            col = lax.rem(p, n * ROWS // BLK)
            row = p // (n * ROWS // BLK)
            at_kv = pl.ds(0, 2)
        else:
            halves = n * ROWS // BLK // 2
            col = lax.rem(p, halves)
            row = p // (2 * halves)
            at_kv = pl.ds(lax.rem(p // halves, 2), 1)
        return at_kv, pl.ds(pl.multiple_of(row * ROWS, ROWS), ROWS), pl.ds(
            pl.multiple_of(col * cols, 128), cols
        )

    load_k = pltpu.make_async_copy(ks_hbm, kv.at[:, 0], load_sem.at[0])
    load_v = pltpu.make_async_copy(vs_hbm, kv.at[:, 1], load_sem.at[1])
    load_k.start()
    load_v.start()
    loads = [
        pltpu.make_async_copy(a, b, load_sem.at[4 + i])
        for i, (a, b) in enumerate((
            (k_hbm, k_ref), (sel_hbm, sel_ref), (v_hbm, v_ref), (q_hbm, q_ref), (qs_hbm, qs_ref)))
    ]
    for c in loads:
        c.start()
    ek_ref = sel_ref.at[pl.ds(0, 2 * FPAD)]
    eq_ref = sel_ref.at[pl.ds(2 * FPAD, 512)]
    count = count_in[0, 0]
    lane8 = lax.broadcasted_iota(jnp.int32, (8, 128), 1)
    ids = jnp.zeros((8, 128), jnp.int32)
    for i in range(maxb):
        ids = jnp.where(lane8 == i, ids_in[0, i], ids)
    ids_ref[...] = jnp.where(lane8 < count, ids, -1)

    barrier = pltpu.get_barrier_semaphore()
    for off in range(1, n):
        pl.semaphore_signal(barrier, inc=1, device_id={"files": peer(off)}, device_id_type=MESH)

    @pl.when(has_prev)
    def _():
        pl.semaphore_signal(barrier, inc=1, device_id={"seq": z - 1}, device_id_type=MESH)

    @pl.when(has_next)
    def _():
        pl.semaphore_signal(barrier, inc=1, device_id={"seq": z + 1}, device_id_type=MESH)

    neighbours = (z + nz - 1) // nz + (2 * nz - 2 - z) // nz
    pl.semaphore_wait(barrier, n - 1 + neighbours)

    id_copies = []
    for off in range(1, n):
        c = pltpu.make_async_remote_copy(
            src_ref=ids_ref, dst_ref=tbl.at[me], send_sem=ids_send.at[off], recv_sem=ids_recv.at[off],
            device_id={"files": peer(off)}, device_id_type=MESH)
        c.start()
        id_copies.append(c)
    tbl[me] = ids_ref[...]
    load_k.wait()
    load_v.wait()
    first = []
    for off in range(1, n):
        to = peer(off)
        at_kv, at_row, at_col = piece(to)
        c = pltpu.make_async_remote_copy(
            src_ref=kv.at[:, at_kv, at_row, at_col], dst_ref=pieces.at[pl.ds(me * blocks, blocks)],
            send_sem=p1_send.at[off], recv_sem=p1_recv.at[off],
            device_id={"files": to}, device_id_type=MESH)
        c.start()
        first.append(c)
    at_kv, at_row, at_col = piece(me)
    mine = pltpu.make_async_copy(
        kv.at[:, at_kv, at_row, at_col], pieces.at[pl.ds(me * blocks, blocks)], load_sem.at[2])
    mine.start()

    lanes_in = heads * FEAT
    qp[...] = jnp.zeros_like(qp)
    kp[...] = jnp.zeros_like(kp)
    for c in loads:
        c.wait()
    qp[:, :lanes_in] = q_ref[...].T
    kp[:, :lanes_in] = k_ref[...].T

    def head_tile(ref, h):
        lane = lax.broadcasted_iota(jnp.int32, (tokens, 128), 1)
        start = pl.multiple_of((h // 8) * 128, 128)
        tile = ref[:, pl.ds(start, 128)]
        low = lax.rem(h, 8) * FEAT
        inside = (lane >= low) & (lane < low + FEAT)
        return tile, jnp.where(inside, tile, jnp.zeros_like(tile))

    def lane_is(h, rows):
        return lax.broadcasted_iota(jnp.int32, (rows, 128), 1) == h

    def columns(h):
        return pl.ds(pl.multiple_of(h * HD, HD), HD)

    n_local[...] = jnp.zeros_like(n_local)

    def state_of(h):
        _, km = head_tile(kp, h)
        both = nt(ek_ref[...], km)
        row = lax.broadcasted_iota(jnp.int32, (FPAD, tokens), 0)
        feat = jnp.where(row == 0, 1.0, both[:FPAD]) * jnp.where(row < 1 + FEAT, 1.0, both[FPAD:])
        ones = jnp.where(lane_is(h, tokens), 1.0, 0.0).astype(BF16)
        right = jnp.concatenate([v_ref[:, columns(h)], ones], axis=1)
        made = nn(feat.astype(BF16), right)
        local[h] = made[:, :HD]
        return made[:, HD:]

    def states(i, carry):
        n_local[...] += state_of(2 * i) + state_of(2 * i + 1)
        return carry

    lax.fori_loop(0, heads // 2, states, 0)

    groups = heads // GROUP

    def norm_copy():
        return pltpu.make_async_remote_copy(
            src_ref=n_send, dst_ref=n_recv, send_sem=nm_send, recv_sem=nm_recv,
            device_id={"seq": lax.rem(z + 1, nz)}, device_id_type=MESH)

    def state_copy(g):
        at = pl.ds(g * GROUP, GROUP)
        return pltpu.make_async_remote_copy(
            src_ref=s_send.at[at], dst_ref=s_recv.at[at], send_sem=st_send.at[g], recv_sem=st_recv.at[g],
            device_id={"seq": lax.rem(z + 1, nz)}, device_id_type=MESH)

    @pl.when(z == 0)
    def _():
        n_recv[...] = jnp.zeros_like(n_recv)
        s_recv[...] = jnp.zeros_like(s_recv)

    @pl.when(has_prev)
    def _():
        norm_copy().wait_recv()

    @pl.when(has_next)
    def _():
        n_send[...] = n_recv[...] + n_local[...]
        norm_copy().start()

    def pass_on(g):
        at = pl.ds(g * GROUP, GROUP)

        @pl.when(has_prev)
        def _():
            state_copy(g).wait_recv()

        @pl.when(has_next)
        def _():
            s_send[at] = (s_recv[at].astype(F32) + local[at]).astype(BF16)
            state_copy(g).start()

    def lin_head(h, norms):
        _, qm = head_tile(qp, h)
        k_tile, _ = head_tile(kp, h)
        s = nt(qm, k_tile) * 0.25
        t_at = lax.broadcasted_iota(jnp.int32, (tokens, tokens), 0)
        s_at = lax.broadcasted_iota(jnp.int32, (tokens, tokens), 1)
        w = jnp.where(s_at <= t_at, 1.0 + s * (1.0 + 0.5 * s), 0.0)
        num = nn(w.astype(BF16), v_ref[:, columns(h)])
        both = nt(qm, eq_ref[...])
        lane = lax.broadcasted_iota(jnp.int32, (tokens, 256), 1)
        feat = jnp.where(lane == 0, 1.0, both[:, :256]) * jnp.where(lane < 1 + FEAT, 1.0, both[:, 256:])
        which = lane_is(h, FPAD) | lane_is(h + 64, FPAD)
        right = jnp.concatenate([s_recv[h], jnp.where(which, norms, jnp.zeros_like(norms))], axis=1)
        far = nn(feat[:, :FPAD].astype(BF16), right)
        den = jnp.sum(w, axis=1, keepdims=True) + jnp.sum(far[:, HD:], axis=1, keepdims=True)
        lin_ref[:, columns(h)] = ((num + far[:, :HD]) / den).astype(BF16)

    def lin_group(g):
        total = n_recv[...]
        high = total.astype(BF16)
        low = (total - high.astype(F32)).astype(BF16)
        norms = jnp.where(
            lax.broadcasted_iota(jnp.int32, (FPAD, 128), 1) < 64,
            high.astype(F32), pltpu.roll(low.astype(F32), 64, 1)).astype(BF16)

        def two(i, carry):
            lin_head(g * GROUP + 2 * i, norms)
            lin_head(g * GROUP + 2 * i + 1, norms)
            return carry

        lax.fori_loop(0, GROUP // 2, two, 0)

    scale = 1.0 / math.sqrt(SM_HD)

    def pairs(part, count):
        def two(i, carry):
            part(2 * i, 0)
            part(2 * i + 1, 0)
            return carry

        lax.fori_loop(0, count // 2, two, 0)

    def own_part(h, carry):
        at = columns(h)
        for b in range(blocks):
            rows = pl.ds(b * BLK, BLK)
            s = nt(qs_ref[rows, at], kv[b, 0, :, at]) * scale
            top = jnp.max(s, axis=1, keepdims=True)
            p = jnp.exp(s - top)
            own_max[h, rows] = top
            own_sum[h, rows] = jnp.sum(p, axis=1, keepdims=True)
            own_num[rows, at] = nn(p.astype(BF16), kv[b, 1, :, at])
        return carry

    def imported_part(h, carry):
        at = columns(h)
        keys = imp[:, 0, :, at].reshape(maxb * BLK, SM_HD)
        s = nt(qs_ref[:, at], keys) * scale
        slot = lax.broadcasted_iota(jnp.int32, (1, maxb * BLK), 1)
        s = jnp.where(slot < count * BLK, s, -jnp.inf)
        top = jnp.maximum(own_max[h], jnp.max(s, axis=1, keepdims=True))
        p = jnp.exp(s - top)
        before = jnp.exp(own_max[h] - top)
        total = own_sum[h] * before + jnp.sum(p, axis=1, keepdims=True)
        values = imp[:, 1, :, at].reshape(maxb * BLK, SM_HD)
        num = own_num[:, at] * before + nn(p.astype(BF16), values)
        soft_ref[:, at] = (num / total).astype(BF16)
        return carry

    second = []

    def exchange():
        for c in id_copies:
            c.wait_recv()
        to_smem = pltpu.make_async_copy(tbl, tbl_s, tbl_sem)
        to_smem.start()
        to_smem.wait()
        for c in first:
            c.wait_recv()
        mine.wait()
        at_kv, at_row, at_col = piece(me)
        for off in range(n):
            to = peer(off)
            for i in range(maxb):
                outgoing[off, i] = pieces[jnp.maximum(tbl_s[to, 0, i], 0)]
            there = imp.at[:, at_kv, at_row, at_col]
            if off == 0:
                c = pltpu.make_async_copy(outgoing.at[0], there, load_sem.at[3])
            else:
                c = pltpu.make_async_remote_copy(
                    src_ref=outgoing.at[off], dst_ref=there,
                    send_sem=p2_send.at[off], recv_sem=p2_recv.at[off],
                    device_id={"files": to}, device_id_type=MESH)
            c.start()
            second.append(c)

    pass_on(0)
    pairs(own_part, sm_heads)
    pass_on(1)
    exchange()
    for g in range(2, groups):
        pass_on(g)
        lin_group(g - 2)
    for g in range(max(groups - 2, 0), groups):
        lin_group(g)

    for c in second:
        if c is second[0]:
            c.wait()
        else:
            c.wait_recv()
    pairs(imported_part, sm_heads)

    for c in id_copies + first + second[1:]:
        c.wait_send()

    @pl.when(has_next)
    def _():
        norm_copy().wait_send()
        for g in range(groups):
            state_copy(g).wait_send()


def body(q_lin, k_lin, v_lin, q_soft, k_soft, v_soft, import_ids, import_counts):
    n, nz = lax.axis_size("files"), lax.axis_size("seq")
    tokens = q_lin.shape[1]
    blocks = tokens // BLK
    heads = q_lin.shape[2] // FEAT
    width, sm_w = v_lin.shape[2], q_soft.shape[2]
    sm_heads = sm_w // SM_HD
    maxb = import_ids.shape[2]
    col_parts = n * ROWS // BLK
    kvs = 2 if sm_w % (128 * col_parts) == 0 else 1
    cols = sm_w // col_parts if kvs == 2 else sm_w * 2 // col_parts
    lanes_in = -(-heads * FEAT // 128) * 128
    picks = jnp.asarray(np.concatenate(selectors()), BF16)
    dims = (n, nz, heads, sm_heads, blocks, maxb, kvs, cols)
    vmem = pl.BlockSpec(memory_space=pltpu.VMEM)
    hbm = pl.BlockSpec(memory_space=pltpu.HBM)
    smem = pl.BlockSpec(memory_space=pltpu.SMEM)
    dma = pltpu.SemaphoreType.DMA
    lin, soft = pl.pallas_call(
        functools.partial(kernel, dims),
        out_shape=(
            jax.ShapeDtypeStruct((tokens, width), BF16),
            jax.ShapeDtypeStruct((tokens, sm_w), BF16),
        ),
        in_specs=[hbm] * 7 + [smem] * 2,
        out_specs=(vmem, vmem),
        scratch_shapes=[
            pltpu.VMEM((heads * FEAT, tokens), BF16),
            pltpu.VMEM((heads * FEAT, tokens), BF16),
            pltpu.VMEM((tokens, width), BF16),
            pltpu.VMEM((tokens, sm_w), BF16),
            pltpu.VMEM(picks.shape, BF16),
            pltpu.VMEM((8, 128), jnp.int32),
            pltpu.VMEM((blocks, 2, BLK, sm_w), BF16),
            pltpu.VMEM((n * blocks, kvs, ROWS, cols), BF16),
            pltpu.VMEM((n, maxb, kvs, ROWS, cols), BF16),
            pltpu.VMEM((maxb, 2, BLK, sm_w), BF16),
            pltpu.VMEM((n, 8, 128), jnp.int32),
            pltpu.SMEM((n, 8, 128), jnp.int32),
            pltpu.VMEM((tokens, lanes_in), BF16),
            pltpu.VMEM((tokens, lanes_in), BF16),
            pltpu.VMEM((heads, FPAD, HD), F32),
            pltpu.VMEM((heads, FPAD, HD), BF16),
            pltpu.VMEM((heads, FPAD, HD), BF16),
            pltpu.VMEM((FPAD, HD), F32),
            pltpu.VMEM((FPAD, HD), F32),
            pltpu.VMEM((FPAD, HD), F32),
            pltpu.VMEM((tokens, sm_w), F32),
            pltpu.VMEM((sm_heads, tokens, 1), F32),
            pltpu.VMEM((sm_heads, tokens, 1), F32),
            dma((9,)), dma((n,)), dma((n,)), dma((n,)), dma((n,)), dma((n,)), dma((n,)),
            dma((heads // GROUP,)), dma((heads // GROUP,)), dma, dma, dma,
        ],
        compiler_params=pltpu.CompilerParams(
            collective_id=0, has_side_effects=True, vmem_limit_bytes=60 * 2**20),
    )(
        q_lin[0].T, k_lin[0].T, v_lin[0], q_soft[0],
        k_soft.reshape(blocks, BLK, sm_w), v_soft.reshape(blocks, BLK, sm_w),
        picks, import_ids[0], import_counts,
    )
    return lin[None], soft[None]


def solution(mesh):
    row = P("files", "seq", None)
    return jax.shard_map(
        body,
        mesh=mesh,
        in_specs=(row,) * 7 + (P("files", "seq"),),
        out_specs=(row, row),
        check_vma=False,
    )
```

```python
import functools
import math

import jax
import jax.numpy as jnp
import numpy as np
from jax import lax
from jax.experimental import pallas as pl
from jax.experimental.pallas import tpu as pltpu
from jax.sharding import PartitionSpec as P

FEAT = 16
FEATS = 153
FPAD = 160
HD = 128
SM_HD = 128
BLK = 128
ROWS = 16
GROUP = 2
MESH = pl.DeviceIdType.MESH
F32 = jnp.float32
BF16 = jnp.bfloat16


def selectors():
    rows, cols = np.triu_indices(FEAT)
    lanes = np.arange(128) % FEAT
    first = np.zeros((FPAD, 128), np.float32)
    second = np.zeros((FPAD, 128), np.float32)
    second_q = np.zeros((FPAD, 128), np.float32)
    for i in range(FEAT):
        first[1 + i] = 0.5 * (lanes == i)
    for f, (i, j) in enumerate(zip(rows, cols)):
        first[1 + FEAT + f] = 0.5 * (lanes == i)
        second[1 + FEAT + f] = 0.5 * (lanes == j)
        second_q[1 + FEAT + f] = (0.25 if i == j else 0.5) * (lanes == j)
    for_k = np.concatenate([first, second])
    gap = np.zeros((256 - FPAD, 128), np.float32)
    for_q = np.concatenate([first, gap, second_q, gap])
    return for_k, for_q


def nt(a, b):
    return lax.dot_general(a, b, (((1,), (1,)), ((), ())), preferred_element_type=F32)


def nn(a, b):
    return lax.dot_general(a, b, (((1,), (0,)), ((), ())), preferred_element_type=F32)


def kernel(
    dims,
    q_hbm, k_hbm, v_hbm, qs_hbm, ks_hbm, vs_hbm, sel_hbm, ids_in, count_in,
    lin_ref, soft_ref,
    q_ref, k_ref, v_ref, qs_ref, sel_ref, ids_ref,
    kv, pieces_a, pieces_b, outgoing, imp, tbl, tbl_s, qp, kp,
    local, s_send, s_recv, n_local, n_send, n_recv, own_num, own_max, own_sum,
    load_sem, ids_send, ids_recv, p1_send, p1_recv, p2_send, p2_recv,
    st_send, st_recv, nm_send, nm_recv, tbl_sem, own_sem,
):
    n, nz, heads, sm_heads, blocks, maxb, kvs, cols = dims
    tokens = blocks * BLK
    me = lax.axis_index("files")
    z = lax.axis_index("seq")
    has_prev = z > 0
    has_next = z < nz - 1

    def peer(off):
        return lax.rem(me + off, n)

    def piece(p):
        if kvs == 2:
            col = lax.rem(p, n * ROWS // BLK)
            row = p // (n * ROWS // BLK)
            at_kv = pl.ds(0, 2)
        else:
            halves = n * ROWS // BLK // 2
            col = lax.rem(p, halves)
            row = p // (2 * halves)
            at_kv = pl.ds(lax.rem(p // halves, 2), 1)
        return at_kv, pl.ds(pl.multiple_of(row * ROWS, ROWS), ROWS), pl.ds(
            pl.multiple_of(col * cols, 128), cols
        )

    load_k = pltpu.make_async_copy(ks_hbm, kv.at[:, 0], load_sem.at[0])
    load_v = pltpu.make_async_copy(vs_hbm, kv.at[:, 1], load_sem.at[1])
    load_k.start()
    load_v.start()
    loads = [
        pltpu.make_async_copy(a, b, load_sem.at[4 + i])
        for i, (a, b) in enumerate((
            (k_hbm, k_ref), (sel_hbm, sel_ref), (v_hbm, v_ref), (q_hbm, q_ref), (qs_hbm, qs_ref)))
    ]
    for c in loads:
        c.start()
    ek_ref = sel_ref.at[pl.ds(0, 2 * FPAD)]
    eq_ref = sel_ref.at[pl.ds(2 * FPAD, 512)]
    count = count_in[0, 0]
    lane8 = lax.broadcasted_iota(jnp.int32, (8, 128), 1)
    ids = jnp.zeros((8, 128), jnp.int32)
    for i in range(maxb):
        ids = jnp.where(lane8 == i, ids_in[0, i], ids)
    ids_ref[...] = jnp.where(lane8 < count, ids, -1)

    barrier = pltpu.get_barrier_semaphore()
    for off in range(1, n):
        pl.semaphore_signal(barrier, inc=1, device_id={"files": peer(off)}, device_id_type=MESH)

    @pl.when(has_prev)
    def _():
        pl.semaphore_signal(barrier, inc=1, device_id={"seq": z - 1}, device_id_type=MESH)

    @pl.when(has_next)
    def _():
        pl.semaphore_signal(barrier, inc=1, device_id={"seq": z + 1}, device_id_type=MESH)

    neighbours = (z + nz - 1) // nz + (2 * nz - 2 - z) // nz
    pl.semaphore_wait(barrier, n - 1 + neighbours)

    id_copies = []
    for off in range(1, n):
        c = pltpu.make_async_remote_copy(
            src_ref=ids_ref, dst_ref=tbl.at[me], send_sem=ids_send.at[off], recv_sem=ids_recv.at[off],
            device_id={"files": peer(off)}, device_id_type=MESH)
        c.start()
        id_copies.append(c)
    tbl[me] = ids_ref[...]
    load_k.wait()
    load_v.wait()
    parts = 2 if cols % 256 == 0 else 1
    pieces = (pieces_a, pieces_b)
    width = cols // parts

    def cut(p, c):
        at_kv, at_row, at_col = piece(p)
        at_col = pl.ds(pl.multiple_of(at_col.start + c * width, 128), width)
        return at_kv, at_row, at_col

    first = []
    for c in range(parts):
        for off in range(1, n):
            to = peer(off)
            at_kv, at_row, at_col = cut(to, c)
            copy = pltpu.make_async_remote_copy(
                src_ref=kv.at[:, at_kv, at_row, at_col], dst_ref=pieces[c].at[pl.ds(me * blocks, blocks)],
                send_sem=p1_send.at[c, off], recv_sem=p1_recv.at[c, off],
                device_id={"files": to}, device_id_type=MESH)
            copy.start()
            first.append(copy)
    mine = []
    for c in range(parts):
        at_kv, at_row, at_col = cut(me, c)
        copy = pltpu.make_async_copy(
            kv.at[:, at_kv, at_row, at_col], pieces[c].at[pl.ds(me * blocks, blocks)], own_sem.at[0, c])
        copy.start()
        mine.append(copy)

    lanes_in = heads * FEAT
    qp[...] = jnp.zeros_like(qp)
    kp[...] = jnp.zeros_like(kp)
    for c in loads:
        c.wait()
    qp[:, :lanes_in] = q_ref[...].T
    kp[:, :lanes_in] = k_ref[...].T

    def head_tile(ref, h):
        lane = lax.broadcasted_iota(jnp.int32, (tokens, 128), 1)
        start = pl.multiple_of((h // 8) * 128, 128)
        tile = ref[:, pl.ds(start, 128)]
        low = lax.rem(h, 8) * FEAT
        inside = (lane >= low) & (lane < low + FEAT)
        return tile, jnp.where(inside, tile, jnp.zeros_like(tile))

    def lane_is(h, rows):
        return lax.broadcasted_iota(jnp.int32, (rows, 128), 1) == h

    def columns(h):
        return pl.ds(pl.multiple_of(h * HD, HD), HD)

    n_local[...] = jnp.zeros_like(n_local)

    def state_of(h):
        _, km = head_tile(kp, h)
        both = nt(ek_ref[...], km)
        row = lax.broadcasted_iota(jnp.int32, (FPAD, tokens), 0)
        feat = jnp.where(row == 0, 1.0, both[:FPAD]) * jnp.where(row < 1 + FEAT, 1.0, both[FPAD:])
        ones = jnp.where(lane_is(h, tokens), 1.0, 0.0).astype(BF16)
        right = jnp.concatenate([v_ref[:, columns(h)], ones], axis=1)
        made = nn(feat.astype(BF16), right)
        local[h] = made[:, :HD]
        return made[:, HD:]

    groups = heads // GROUP

    def norm_copy():
        return pltpu.make_async_remote_copy(
            src_ref=n_send, dst_ref=n_recv, send_sem=nm_send, recv_sem=nm_recv,
            device_id={"seq": lax.rem(z + 1, nz)}, device_id_type=MESH)

    def state_copy(g):
        at = pl.ds(g * GROUP, GROUP)
        return pltpu.make_async_remote_copy(
            src_ref=s_send.at[at], dst_ref=s_recv.at[at], send_sem=st_send.at[g], recv_sem=st_recv.at[g],
            device_id={"seq": lax.rem(z + 1, nz)}, device_id_type=MESH)

    def states(i, carry):
        n_local[...] += state_of(2 * i) + state_of(2 * i + 1)

        @pl.when(z == 0)
        def _():
            at = pl.ds(2 * i, GROUP)
            s_send[at] = local[at].astype(BF16)
            state_copy(i).start()

        return carry

    lax.fori_loop(0, groups, states, 0)

    @pl.when(z == 0)
    def _():
        n_recv[...] = jnp.zeros_like(n_recv)
        s_recv[...] = jnp.zeros_like(s_recv)
        n_send[...] = n_local[...]
        norm_copy().start()

    def forward_norm():
        @pl.when(has_prev)
        def _():
            norm_copy().wait_recv()

        @pl.when(has_prev & has_next)
        def _():
            n_send[...] = n_recv[...] + n_local[...]
            norm_copy().start()

    def forward(g, here):
        at = pl.ds(g * GROUP, GROUP)

        @pl.when(has_prev & has_next & here)
        def _():
            state_copy(g).wait_recv()
            s_send[at] = (s_recv[at].astype(F32) + local[at]).astype(BF16)
            state_copy(g).start()

    def lin_head(h, norms):
        _, qm = head_tile(qp, h)
        k_tile, _ = head_tile(kp, h)
        s = nt(qm, k_tile) * 0.25
        t_at = lax.broadcasted_iota(jnp.int32, (tokens, tokens), 0)
        s_at = lax.broadcasted_iota(jnp.int32, (tokens, tokens), 1)
        w = jnp.where(s_at <= t_at, 1.0 + s * (1.0 + 0.5 * s), 0.0)
        num = nn(w.astype(BF16), v_ref[:, columns(h)])
        both = nt(qm, eq_ref[...])
        lane = lax.broadcasted_iota(jnp.int32, (tokens, 256), 1)
        feat = jnp.where(lane == 0, 1.0, both[:, :256]) * jnp.where(lane < 1 + FEAT, 1.0, both[:, 256:])
        which = lane_is(h, FPAD) | lane_is(h + 64, FPAD)
        right = jnp.concatenate([s_recv[h], jnp.where(which, norms, jnp.zeros_like(norms))], axis=1)
        far = nn(feat[:, :FPAD].astype(BF16), right)
        den = jnp.sum(w, axis=1, keepdims=True) + jnp.sum(far[:, HD:], axis=1, keepdims=True)
        lin_ref[:, columns(h)] = ((num + far[:, :HD]) / den).astype(BF16)

    def lin_group(g):
        @pl.when(z == nz - 1)
        def _():
            state_copy(g).wait_recv()

        total = n_recv[...]
        high = total.astype(BF16)
        low = (total - high.astype(F32)).astype(BF16)
        norms = jnp.where(
            lax.broadcasted_iota(jnp.int32, (FPAD, 128), 1) < 64,
            high.astype(F32), pltpu.roll(low.astype(F32), 64, 1)).astype(BF16)

        def two(i, carry):
            lin_head(g * GROUP + 2 * i, norms)
            lin_head(g * GROUP + 2 * i + 1, norms)
            return carry

        lax.fori_loop(0, GROUP // 2, two, 0)

    scale = 1.0 / math.sqrt(SM_HD)

    def pairs(part, low, high):
        def two(i, carry):
            part(low + 2 * i, 0)
            part(low + 2 * i + 1, 0)
            return carry

        lax.fori_loop(0, (high - low) // 2, two, 0)
        if (high - low) % 2:
            part(high - 1, 0)

    def own_part(h, carry):
        at = columns(h)
        for b in range(blocks):
            rows = pl.ds(b * BLK, BLK)
            s = nt(qs_ref[rows, at], kv[b, 0, :, at]) * scale
            top = jnp.max(s, axis=1, keepdims=True)
            p = jnp.exp(s - top)
            own_max[h, rows] = top
            own_sum[h, rows] = jnp.sum(p, axis=1, keepdims=True)
            own_num[rows, at] = nn(p.astype(BF16), kv[b, 1, :, at])
        return carry

    def imported_part(h, carry):
        at = columns(h)
        keys = imp[:, 0, :, at].reshape(maxb * BLK, SM_HD)
        s = nt(qs_ref[:, at], keys) * scale
        slot = lax.broadcasted_iota(jnp.int32, (1, maxb * BLK), 1)
        s = jnp.where(slot < count * BLK, s, -jnp.inf)
        top = jnp.maximum(own_max[h], jnp.max(s, axis=1, keepdims=True))
        p = jnp.exp(s - top)
        before = jnp.exp(own_max[h] - top)
        total = own_sum[h] * before + jnp.sum(p, axis=1, keepdims=True)
        values = imp[:, 1, :, at].reshape(maxb * BLK, SM_HD)
        num = own_num[:, at] * before + nn(p.astype(BF16), values)
        soft_ref[:, at] = (num / total).astype(BF16)
        return carry

    second = [[] for _ in range(parts)]

    def exchange(c):
        if c == 0:
            for copy in id_copies:
                copy.wait_recv()
            to_smem = pltpu.make_async_copy(tbl, tbl_s, tbl_sem)
            to_smem.start()
            to_smem.wait()
        for copy in first[c * (n - 1):(c + 1) * (n - 1)]:
            copy.wait_recv()
        mine[c].wait()
        at_kv, at_row, at_col = cut(me, c)
        there = imp.at[:, at_kv, at_row, at_col]
        for off in list(range(1, n)) + [0]:
            to = peer(off)
            for i in range(maxb):
                outgoing[c, off, i] = pieces[c][jnp.maximum(tbl_s[to, 0, i], 0)]
            if off == 0:
                copy = pltpu.make_async_copy(outgoing.at[c, 0], there, own_sem.at[1, c])
            else:
                copy = pltpu.make_async_remote_copy(
                    src_ref=outgoing.at[c, off], dst_ref=there,
                    send_sem=p2_send.at[c, off], recv_sem=p2_recv.at[c, off],
                    device_id={"files": to}, device_id_type=MESH)
            copy.start()
            second[c].append(copy)

    always = z >= 0
    pairs(own_part, 0, sm_heads)
    exchange(0)
    forward_norm()
    forward(0, z < 3)
    forward(1, z < 2)
    for c in range(1, parts):
        exchange(c)
    forward(0, z >= 3)
    forward(1, z >= 2)
    for g in range(2, groups):
        forward(g, always)
        if g >= 4:
            lin_group(g - 4)
    for g in range(groups - 4, groups):
        lin_group(g)

    for c in range(parts):
        for copy in second[c][:-1]:
            copy.wait_recv()
        second[c][-1].wait()
        if parts == 2:
            pairs(imported_part, c * sm_heads // 2, (c + 1) * sm_heads // 2)
    if parts == 1:
        pairs(imported_part, 0, sm_heads)

    for copy in id_copies + first:
        copy.wait_send()
    for c in range(parts):
        for copy in second[c][:-1]:
            copy.wait_send()

    @pl.when(has_next)
    def _():
        norm_copy().wait_send()
        for g in range(groups):
            state_copy(g).wait_send()


def body(q_lin, k_lin, v_lin, q_soft, k_soft, v_soft, import_ids, import_counts):
    n, nz = lax.axis_size("files"), lax.axis_size("seq")
    tokens = q_lin.shape[1]
    blocks = tokens // BLK
    heads = q_lin.shape[2] // FEAT
    width, sm_w = v_lin.shape[2], q_soft.shape[2]
    sm_heads = sm_w // SM_HD
    maxb = import_ids.shape[2]
    col_parts = n * ROWS // BLK
    kvs = 2 if sm_w % (128 * col_parts) == 0 else 1
    cols = sm_w // col_parts if kvs == 2 else sm_w * 2 // col_parts
    parts = 2 if cols % 256 == 0 else 1
    lanes_in = -(-heads * FEAT // 128) * 128
    picks = jnp.asarray(np.concatenate(selectors()), BF16)
    dims = (n, nz, heads, sm_heads, blocks, maxb, kvs, cols)
    vmem = pl.BlockSpec(memory_space=pltpu.VMEM)
    hbm = pl.BlockSpec(memory_space=pltpu.HBM)
    smem = pl.BlockSpec(memory_space=pltpu.SMEM)
    dma = pltpu.SemaphoreType.DMA
    lin, soft = pl.pallas_call(
        functools.partial(kernel, dims),
        out_shape=(
            jax.ShapeDtypeStruct((tokens, width), BF16),
            jax.ShapeDtypeStruct((tokens, sm_w), BF16),
        ),
        in_specs=[hbm] * 7 + [smem] * 2,
        out_specs=(vmem, vmem),
        scratch_shapes=[
            pltpu.VMEM((heads * FEAT, tokens), BF16),
            pltpu.VMEM((heads * FEAT, tokens), BF16),
            pltpu.VMEM((tokens, width), BF16),
            pltpu.VMEM((tokens, sm_w), BF16),
            pltpu.VMEM(picks.shape, BF16),
            pltpu.VMEM((8, 128), jnp.int32),
            pltpu.VMEM((blocks, 2, BLK, sm_w), BF16),
            pltpu.VMEM((n * blocks, kvs, ROWS, cols // parts), BF16),
            pltpu.VMEM((n * blocks if parts == 2 else 1, kvs, ROWS, cols // parts), BF16),
            pltpu.VMEM((parts, n, maxb, kvs, ROWS, cols // parts), BF16),
            pltpu.VMEM((maxb, 2, BLK, sm_w), BF16),
            pltpu.VMEM((n, 8, 128), jnp.int32),
            pltpu.SMEM((n, 8, 128), jnp.int32),
            pltpu.VMEM((tokens, lanes_in), BF16),
            pltpu.VMEM((tokens, lanes_in), BF16),
            pltpu.VMEM((heads, FPAD, HD), F32),
            pltpu.VMEM((heads, FPAD, HD), BF16),
            pltpu.VMEM((heads, FPAD, HD), BF16),
            pltpu.VMEM((FPAD, HD), F32),
            pltpu.VMEM((FPAD, HD), F32),
            pltpu.VMEM((FPAD, HD), F32),
            pltpu.VMEM((tokens, sm_w), F32),
            pltpu.VMEM((sm_heads, tokens, 1), F32),
            pltpu.VMEM((sm_heads, tokens, 1), F32),
            dma((9,)), dma((n,)), dma((n,)), dma((parts, n)), dma((parts, n)), dma((parts, n)), dma((parts, n)),
            dma((heads // GROUP,)), dma((heads // GROUP,)), dma, dma, dma, dma((2, parts)),
        ],
        compiler_params=pltpu.CompilerParams(
            collective_id=0, has_side_effects=True, vmem_limit_bytes=60 * 2**20),
    )(
        q_lin[0].T, k_lin[0].T, v_lin[0], q_soft[0],
        k_soft.reshape(blocks, BLK, sm_w), v_soft.reshape(blocks, BLK, sm_w),
        picks, import_ids[0], import_counts,
    )
    return lin[None], soft[None]


def solution(mesh):
    row = P("files", "seq", None)
    return jax.shard_map(
        body,
        mesh=mesh,
        in_specs=(row,) * 7 + (P("files", "seq"),),
        out_specs=(row, row),
        check_vma=False,
    )
```
